32 devices in a mesh: ctx: 8 (over z, x), head: 4 (over y, core).
Axes of the slice: x: 2, y: 2, z: 4, core: 2. Of those that a mesh axis runs over, the one named last changes fastest.
Arguments:
- projected: bfloat16 [3, 4096, 4096], P(None, ('ctx', 'head')), may hold values from -2.5 to 2.5
- conv_filter: float32 [3, 4, 4096], replicated, may hold values from -2.7 to 2.7
- frequencies: bfloat16 [32, 128, 256], replicated, may hold values from -5 to 5
Outputs:
- attended: bfloat16 [4096, 4096], P(('ctx', 'head'))
The draws below stay inside these ranges and needn't reach their ends.
All inputs are finite; a program needn't handle non-finite values.
Results may differ from the reference program's by a relative error of at most 0.013.
Values may be sent and summed in bfloat16 or wider, within the bound.
A program may use at most 384 MiB of HBM per device.

```python
import jax
import jax.numpy as jnp
from jax import lax

H = 32
DH = 128
M = 256
KC = 4
BLOCK = 512
D = 4096
TOKENS = 4096


def shard_levels(stream_key, shape, cuts, least, top_value):
    loudness, own = 1.0, jax.random.fold_in(stream_key, 6)
    for axis_at, shards_of in cuts:
        heights = jnp.exp(jax.random.uniform(jax.random.fold_in(own, axis_at), (shards_of,), jnp.float32, least / len(cuts), top_value / len(cuts)))
        loudness = loudness * jnp.repeat(heights, shape[axis_at] // shards_of).reshape([-1 if axis == axis_at else 1 for axis in range(len(shape))])
    return loudness


def bell_draw(key, extent, spread, reach, cuts=(), held_as=jnp.bfloat16):
    level = shard_levels(key, extent, cuts, -0.22, 0.18) if cuts else 1.0
    result = jax.random.normal(key, extent, jnp.float32) * spread * level
    return jnp.minimum(jnp.maximum(result, -reach), reach).astype(held_as)


def setup_inputs(seed: int = 0) -> dict:
    key_list = jax.random.split(jax.random.key(seed), 4)
    return {
        "projected": bell_draw(key_list[0], (3, TOKENS, D), 1.0, 2.5, ((1, 32),)),
        "conv_filter": bell_draw(key_list[1], (3, KC, D), 0.45, 2.7, (), jnp.float32),
        "frequencies": bell_draw(key_list[2], (H, DH, M), 1.0, 5.0),
    }


def reference(projected, conv_filter, frequencies):
    block_count = TOKENS // BLOCK
    causal = jnp.arange(BLOCK)[:, None] >= jnp.arange(BLOCK)[None, :]
    feature_scale = DH ** -0.25

    def advance(carried, pieces):
        running_state_sum, key_total = carried
        block_of_queries, block_of_keys, value_block = pieces
        scores = jnp.dot(block_of_queries, block_of_keys.T, preferred_element_type=jnp.float32)
        scores = jnp.where(causal, scores, 0.0).astype(jnp.bfloat16)
        query_wide = block_of_queries.astype(jnp.float32)
        numerator = jnp.dot(scores, value_block, preferred_element_type=jnp.float32)
        numerator = numerator + jnp.dot(query_wide, running_state_sum, precision=lax.Precision.HIGHEST)
        denominator = jnp.sum(scores.astype(jnp.float32), axis=1) + jnp.dot(query_wide, key_total, precision=lax.Precision.HIGHEST)
        attended_output = (numerator / denominator[:, None]).astype(jnp.bfloat16)
        running_state_sum = running_state_sum + jnp.dot(block_of_keys.T, value_block, preferred_element_type=jnp.float32)
        key_total = key_total + jnp.sum(block_of_keys.astype(jnp.float32), axis=0)
        return (running_state_sum, key_total), attended_output

    def one_head(head_index):
        col_start = head_index * DH
        columns = lax.dynamic_slice_in_dim(projected, col_start, DH, 2).astype(jnp.float32)
        conv_taps = lax.dynamic_slice_in_dim(conv_filter, col_start, DH, 2)
        padded = jnp.pad(columns, ((0, 0), (KC - 1, 0), (0, 0)))
        summed = jnp.zeros_like(columns)
        for offset in range(KC):
            summed = summed + conv_taps[:, offset][:, None, :] * padded[:, KC - 1 - offset:KC - 1 - offset + TOKENS, :]
        conved = summed.astype(jnp.bfloat16)
        head_omega = frequencies[head_index]
        query_map = jnp.exp(jnp.dot(conved[0], head_omega, preferred_element_type=jnp.float32) * feature_scale).astype(jnp.bfloat16)
        keys_wide = conved[1].astype(jnp.float32)
        halfnorm = jnp.sum(keys_wide * keys_wide, axis=1, keepdims=True) * (0.5 * feature_scale * feature_scale)
        key_map = jnp.exp(jnp.dot(conved[1], head_omega, preferred_element_type=jnp.float32) * feature_scale - halfnorm).astype(jnp.bfloat16)
        initial = (jnp.zeros((M, DH), jnp.float32), jnp.zeros((M,), jnp.float32))
        pieces = (query_map.reshape(block_count, BLOCK, M), key_map.reshape(block_count, BLOCK, M), conved[2].reshape(block_count, BLOCK, DH))
        finals, output_list = lax.scan(advance, initial, pieces)
        return output_list.reshape(TOKENS, DH)

    per_head = lax.map(one_head, jnp.arange(H, dtype=jnp.int32))
    return jnp.transpose(per_head, (1, 0, 2)).reshape(TOKENS, H * DH)
```

```python
import functools

import jax
import jax.numpy as jnp
from jax import lax
from jax.experimental import pallas as pl
from jax.experimental.pallas import tpu as pltpu
from jax.sharding import PartitionSpec as P

DH = 128
M = 256
KC = 4
CORES = 2
RIM = 16
SROWS = DH + 16
MESH = pl.DeviceIdType.MESH


def kernel(
    plan,
    proj, filt, freq, out,
    x_all, omega, kf, vals, qf, intra, s_send, s_recv, chain_in, chain_out, r_send, r_recv, outb,
    load_sem, freq_sem, ex_send, ex_recv, rim_send, rim_recv,
    ss_sem, sr_sem, cs_sem, cr_sem, rs_sem, rr_sem, os_sem, or_sem, ol_sem,
):
    X, Y, Z = plan
    G = X * Y
    rows = proj.shape[1]
    half = proj.shape[2] // CORES
    J = half // DH // G
    T = CORES * rows
    wide = G * DH
    scale = DH ** (-0.25)

    c = lax.axis_index("ctx")
    hd = lax.axis_index("head")
    y, core = hd // CORES, hd % CORES
    z, x = c // X, c % X
    me = x * Y + y
    other = 1 - core
    chip = c * Y + y
    chips = X * Y * Z

    def member(g):
        return (z * X + g // Y, (g % Y) * CORES + core)

    def at_chip(n, k):
        return (n // Y, (n % Y) * CORES + k)

    mate = (c, y * CORES + other)
    has_next = (core == 1) & (chip < chips - 1)
    has_prev = chip > 0

    barrier = pltpu.get_barrier_semaphore()

    def greet(dev):
        pl.semaphore_signal(barrier, inc=1, device_id=dev, device_id_type=MESH)

    greet(mate)
    for g in range(G):
        pl.when(g != me)(lambda g=g: greet(member(g)))
    pl.when(z > 0)(lambda: greet((c - X, hd)))
    pl.when(z < Z - 1)(lambda: greet((c + X, hd)))
    for k in range(CORES):
        pl.when(has_next)(lambda k=k: greet(at_chip(chip + 1, k)))
    pl.when(has_prev)(lambda: greet(at_chip(chip - 1, 1)))

    my_cols = pl.ds(pl.multiple_of(core * half, half), half)
    mate_cols = pl.ds(pl.multiple_of(other * half, half), half)
    my_rows = pl.ds(pl.multiple_of(RIM + core * rows, 16), rows)
    mate_rows = pl.ds(pl.multiple_of(RIM + other * rows, 16), rows)

    def load(a):
        return pltpu.make_async_copy(
            proj.at[a, :, my_cols], x_all.at[a, my_rows, :], load_sem.at[a]
        )

    def exchange(a):
        return pltpu.make_async_remote_copy(
            proj.at[a, :, mate_cols], x_all.at[a, my_rows, :],
            ex_send.at[a], ex_recv.at[a], device_id=mate, device_id_type=MESH,
        )

    def rim(a, k):
        return pltpu.make_async_remote_copy(
            proj.at[a, pl.ds(rows - RIM, RIM), pl.ds(k * half, half)],
            x_all.at[a, pl.ds(0, RIM), :],
            rim_send.at[a, k], rim_recv.at[a],
            device_id=at_chip(chip + 1, k), device_id_type=MESH,
        )

    omega_copy = pltpu.make_async_copy(
        freq.at[pl.ds(core * (half // DH), half // DH)], omega, freq_sem
    )
    for a in (1, 2, 0):
        load(a).start()
    omega_copy.start()

    @pl.when(jnp.logical_not(has_prev))
    def _():
        x_all[:, pl.ds(0, RIM), :] = jnp.zeros((3, RIM, half), x_all.dtype)

    greeted = (
        G + (z > 0).astype(jnp.int32) + (z < Z - 1).astype(jnp.int32)
        + CORES * has_next.astype(jnp.int32) + has_prev.astype(jnp.int32)
    )
    pl.semaphore_wait(barrier, greeted)

    for a in (1, 2, 0):
        for k in range(CORES):
            pl.when(has_next)(lambda a=a, k=k: rim(a, k).start())
        exchange(a).start()

    def arrive(a):
        load(a).wait()
        exchange(a).wait_recv()

        @pl.when(has_prev)
        def _():
            pltpu.make_async_copy(
                x_all.at[a, pl.ds(0, RIM), :], x_all.at[a, pl.ds(0, RIM), :], rim_recv.at[a]
            ).wait()

    def conv(a, h):
        cols = pl.ds(pl.multiple_of(h * DH, DH), DH)
        taps = filt[a, :, pl.ds(pl.multiple_of(core * half + h * DH, DH), DH)]
        data = x_all[a, :, cols].astype(jnp.float32)
        total = taps[0:1] * data[RIM:]
        for j in range(1, KC):
            total = total + taps[j : j + 1] * pltpu.roll(data, j, 0)[RIM:]
        return total.astype(jnp.bfloat16)

    def s_copy(j, o):
        return pltpu.make_async_remote_copy(
            s_send.at[j, o], s_recv.at[j, me], ss_sem.at[j, o], sr_sem.at[j, me],
            device_id=member(o), device_id_type=MESH,
        )

    def s_arrival(j, g):
        return pltpu.make_async_remote_copy(
            s_send.at[j, g], s_recv.at[j, g], ss_sem.at[j, g], sr_sem.at[j, g],
            device_id=member(g), device_id_type=MESH,
        )

    def r_copy(j, g):
        return pltpu.make_async_remote_copy(
            r_send.at[j, g], r_recv.at[j, me], rs_sem.at[j, g], rr_sem.at[j, me],
            device_id=member(g), device_id_type=MESH,
        )

    def r_arrival(j, o):
        return pltpu.make_async_remote_copy(
            r_send.at[j, o], r_recv.at[j, o], rs_sem.at[j, o], rr_sem.at[j, o],
            device_id=member(o), device_id_type=MESH,
        )

    def chain(j):
        return pltpu.make_async_remote_copy(
            chain_out.at[j], chain_in.at[j], cs_sem.at[j], cr_sem.at[j],
            device_id=(c + X, hd), device_id_type=MESH,
        )

    def keys_and_sums(j, o):
        h = j * G + o
        k = conv(1, h)
        v = conv(2, h)
        wide_k = k.astype(jnp.float32)
        norm = jnp.sum(wide_k * wide_k, axis=1, keepdims=True) * (0.5 * scale * scale)
        part = jnp.dot(k, omega[h], preferred_element_type=jnp.float32)
        feats = jnp.exp(part * scale - norm).astype(jnp.bfloat16)
        kf[h] = feats
        vals[h] = v
        joined = jnp.concatenate([v, jnp.ones_like(v)], axis=1)
        sums = lax.dot_general(
            joined, feats, (((0,), (0,)), ((), ())), preferred_element_type=jnp.float32
        )
        sums = sums[:SROWS].astype(jnp.bfloat16)

        @pl.when(o == me)
        def _():
            s_recv[j, o] = sums

        @pl.when(o != me)
        def _():
            s_send[j, o] = sums
            s_copy(j, o).start()

    def own(j):
        def await_sums(g, _):
            pl.when(g != me)(lambda: s_arrival(j, g).wait_recv())
            return 0

        lax.fori_loop(0, G, await_sums, 0)
        total = s_recv[j, 0].astype(jnp.float32)
        for g in range(1, G):
            total = total + s_recv[j, g].astype(jnp.float32)

        @pl.when(z == 0)
        def _():
            chain_in[j] = jnp.zeros((SROWS, M), jnp.bfloat16)

        @pl.when(z > 0)
        def _():
            chain(j).wait_recv()

        before = chain_in[j].astype(jnp.float32)

        @pl.when(z < Z - 1)
        def _():
            chain_out[j] = (before + total).astype(jnp.bfloat16)
            chain(j).start()

        running = before
        for g in range(G):
            piece = running.astype(jnp.bfloat16)

            @pl.when(g == me)
            def _():
                r_recv[j, g] = piece

            @pl.when(g != me)
            def _():
                r_send[j, g] = piece
                r_copy(j, g).start()

            if g < G - 1:
                running = running + s_recv[j, g].astype(jnp.float32)

    def within(j, o):
        h = j * G + o
        q = conv(0, h)
        part = jnp.dot(q, omega[h], preferred_element_type=jnp.float32)
        feats = jnp.exp(part * scale).astype(jnp.bfloat16)
        qf[h] = feats
        scores = lax.dot_general(
            feats, kf[h], (((1,), (1,)), ((), ())), preferred_element_type=jnp.float32
        )
        at = lax.broadcasted_iota(jnp.int32, (T, T), 0)
        of = lax.broadcasted_iota(jnp.int32, (T, T), 1)
        scores = jnp.where(at >= of, scores, 0.0).astype(jnp.bfloat16)
        v = vals[h]
        joined = jnp.concatenate([v, jnp.ones_like(v)], axis=1)
        intra[h] = jnp.dot(scores, joined, preferred_element_type=jnp.float32)

    def finish(j, o):
        h = j * G + o
        pl.when(o != me)(lambda: r_arrival(j, o).wait_recv())
        state = r_recv[j, o]
        joined = jnp.concatenate([state[:DH]] + [state[DH:]] * (DH // 16), axis=0)
        both = intra[h] + lax.dot_general(
            qf[h], joined, (((1,), (1,)), ((), ())), preferred_element_type=jnp.float32
        )
        result = (both[:, :DH] / both[:, DH:]).astype(jnp.bfloat16)
        outb[:, pl.ds(pl.multiple_of(h * DH, DH), DH)] = result

    def out_cols(j):
        return pl.ds(pl.multiple_of(j * wide, wide), wide)

    def out_remote(j):
        return pltpu.make_async_remote_copy(
            outb.at[pl.ds(pl.multiple_of(other * rows, rows), rows), out_cols(j)],
            out.at[:, pl.ds(pl.multiple_of(core * half + j * wide, wide), wide)],
            os_sem.at[j], or_sem.at[j], device_id=mate, device_id_type=MESH,
        )

    def out_local(j):
        return pltpu.make_async_copy(
            outb.at[pl.ds(pl.multiple_of(core * rows, rows), rows), out_cols(j)],
            out.at[:, pl.ds(pl.multiple_of(core * half + j * wide, wide), wide)],
            ol_sem.at[j],
        )

    def over(count, body):
        def step(i, _):
            body(i)
            return 0

        lax.fori_loop(0, count, step, 0)

    omega_copy.wait()
    arrive(1)
    arrive(2)
    over(J, lambda j: over(G, lambda o: keys_and_sums(j, o)))
    arrive(0)

    def middle(j):
        own(j)
        over(G, lambda o: within(j, o))

    over(J, middle)

    def last(j):
        over(G, lambda o: finish(j, o))
        out_remote(j).start()
        out_local(j).start()

    over(J, last)

    for a in range(3):
        exchange(a).wait_send()
        for k in range(CORES):
            pl.when(has_next)(lambda a=a, k=k: rim(a, k).wait_send())

    def drain(j):
        def one(g):
            @pl.when(g != me)
            def _():
                s_copy(j, g).wait_send()
                r_copy(j, g).wait_send()

        over(G, one)
        pl.when(z < Z - 1)(lambda: chain(j).wait_send())
        out_remote(j).wait()
        out_local(j).wait()

    over(J, drain)


def plan_of(ctx_size, head_size):
    along_x = 1
    while along_x * along_x * 4 <= ctx_size:
        along_x *= 2
    return along_x, head_size // CORES, ctx_size // along_x


def per_device(projected, conv_filter, frequencies):
    plan = plan_of(lax.axis_size("ctx"), lax.axis_size("head"))
    rows, width = projected.shape[1], projected.shape[2]
    half = width // CORES
    heads = half // DH
    group = plan[0] * plan[1]
    slots = heads // group
    T = CORES * rows
    bf16 = jnp.bfloat16
    dma = pltpu.SemaphoreType.DMA
    return pl.pallas_call(
        functools.partial(kernel, plan),
        out_shape=jax.ShapeDtypeStruct((rows, width), bf16),
        in_specs=[
            pl.BlockSpec(memory_space=pl.ANY),
            pl.BlockSpec(memory_space=pltpu.VMEM),
            pl.BlockSpec(memory_space=pl.ANY),
        ],
        out_specs=pl.BlockSpec(memory_space=pl.ANY),
        scratch_shapes=[
            pltpu.VMEM((3, RIM + T, half), bf16),
            pltpu.VMEM((heads, DH, M), bf16),
            pltpu.VMEM((heads, T, M), bf16),
            pltpu.VMEM((heads, T, DH), bf16),
            pltpu.VMEM((heads, T, M), bf16),
            pltpu.VMEM((heads, T, 2 * DH), jnp.float32),
            pltpu.VMEM((slots, group, SROWS, M), bf16),
            pltpu.VMEM((slots, group, SROWS, M), bf16),
            pltpu.VMEM((slots, SROWS, M), bf16),
            pltpu.VMEM((slots, SROWS, M), bf16),
            pltpu.VMEM((slots, group, SROWS, M), bf16),
            pltpu.VMEM((slots, group, SROWS, M), bf16),
            pltpu.VMEM((T, half), bf16),
            dma((3,)), dma, dma((3,)), dma((3,)), dma((3, CORES)), dma((3,)),
            dma((slots, group)), dma((slots, group)),
            dma((slots,)), dma((slots,)),
            dma((slots, group)), dma((slots, group)),
            dma((slots,)), dma((slots,)), dma((slots,)),
        ],
        compiler_params=pltpu.CompilerParams(
            collective_id=0, has_side_effects=True, vmem_limit_bytes=48 * 1024 * 1024
        ),
        cost_estimate=pl.CostEstimate(
            flops=2_000_000_000, bytes_accessed=8_000_000, transcendentals=2_000_000
        ),
    )(projected, conv_filter, frequencies)


def solution(mesh):
    placed = (P(None, ("ctx", "head"), None), P(), P())
    return jax.shard_map(
        per_device, mesh=mesh, in_specs=placed, out_specs=P(("ctx", "head"), None), check_vma=False
    )
```

```python
import functools

import jax
import jax.numpy as jnp
from jax import lax
from jax.experimental import pallas as pl
from jax.experimental.pallas import tpu as pltpu
from jax.sharding import PartitionSpec as P

DH = 128
M = 256
KC = 4
CORES = 2
RIM = 16
SROWS = 2 * DH + 16
MESH = pl.DeviceIdType.MESH


def kernel(
    plan,
    proj, filt, freq, out,
    x_all, tail, packed, rim_in, taps_all, omega, kf, vals, qf, intra, s_send, s_recv, chain_in, chain_out, r_send, r_recv, outb,
    load_sem, freq_sem, filt_sem, tail_sem, ex_send, ex_recv, rim_send, rim_recv,
    ss_sem, sr_sem, cs_sem, cr_sem, rs_sem, rr_sem, os_sem, or_sem, ol_sem,
):
    X, Y, Z = plan
    G = X * Y
    rows = proj.shape[1]
    half = proj.shape[2] // CORES
    J = half // DH // G
    T = CORES * rows
    wide = G * DH
    scale = DH ** (-0.25)

    c = lax.axis_index("ctx")
    hd = lax.axis_index("head")
    y, core = hd // CORES, hd % CORES
    z, x = c // X, c % X
    me = x * Y + y
    other = 1 - core
    chip = c * Y + y
    chips = X * Y * Z

    def member(g):
        return (z * X + g // Y, (g % Y) * CORES + core)

    def at_chip(n, k):
        return (n // Y, (n % Y) * CORES + k)

    mate = (c, y * CORES + other)
    has_next = (core == 1) & (chip < chips - 1)
    has_prev = chip > 0

    barrier = pltpu.get_barrier_semaphore()

    def greet(dev):
        pl.semaphore_signal(barrier, inc=1, device_id=dev, device_id_type=MESH)

    greet(mate)
    for g in range(G):
        pl.when(g != me)(lambda g=g: greet(member(g)))
    pl.when(z > 0)(lambda: greet((c - X, hd)))
    pl.when(z < Z - 1)(lambda: greet((c + X, hd)))
    for k in range(CORES):
        pl.when(has_next)(lambda k=k: greet(at_chip(chip + 1, k)))
    pl.when(has_prev)(lambda: greet(at_chip(chip - 1, 1)))

    my_cols = pl.ds(pl.multiple_of(core * half, half), half)
    my_rows = pl.ds(pl.multiple_of(RIM + core * rows, 16), rows)

    def load(a):
        return pltpu.make_async_copy(
            proj.at[a, :, my_cols], x_all.at[a, my_rows, :], load_sem.at[a]
        )

    def exchange(a, j):
        far = pl.ds(pl.multiple_of(other * half + j * wide, wide), wide)
        near = pl.ds(pl.multiple_of(j * wide, wide), wide)
        return pltpu.make_async_remote_copy(
            proj.at[a, :, far], x_all.at[a, my_rows, near],
            ex_send.at[a, j], ex_recv.at[a, j], device_id=mate, device_id_type=MESH,
        )

    def rim(k):
        return pltpu.make_async_remote_copy(
            packed.at[:, pl.ds(k * half, half)], rim_in,
            rim_send.at[k], rim_recv,
            device_id=at_chip(chip + 1, k), device_id_type=MESH,
        )

    tail_copy = pltpu.make_async_copy(proj.at[:, pl.ds(rows - RIM, RIM), :], tail, tail_sem)
    taps_copy = pltpu.make_async_copy(filt.at[:, :, my_cols], taps_all, filt_sem)

    omega_copy = pltpu.make_async_copy(
        freq.at[pl.ds(core * (half // DH), half // DH)], omega, freq_sem
    )
    pl.when(has_next)(tail_copy.start)
    load(1).start()
    load(2).start()
    taps_copy.start()
    omega_copy.start()
    load(0).start()

    @pl.when(has_next)
    def _():
        tail_copy.wait()
        row = lax.broadcasted_iota(jnp.int32, (RIM, half), 0)
        for k in range(CORES):
            parts = [tail[a, :, pl.ds(k * half, half)].astype(jnp.float32) for a in range(3)]
            both = jnp.where(row >= RIM - 6, pltpu.roll(parts[1], RIM - 3, 0), pltpu.roll(parts[2], RIM - 6, 0))
            joined = jnp.where(row >= RIM - 3, parts[0], both)
            packed[:, pl.ds(k * half, half)] = joined.astype(packed.dtype)

    @pl.when(jnp.logical_not(has_prev))
    def _():
        rim_in[...] = jnp.zeros((RIM, half), rim_in.dtype)

    greeted = (
        G + (z > 0).astype(jnp.int32) + (z < Z - 1).astype(jnp.int32)
        + CORES * has_next.astype(jnp.int32) + has_prev.astype(jnp.int32)
    )
    pl.semaphore_wait(barrier, greeted)

    for k in range(CORES):
        pl.when(has_next)(lambda k=k: rim(k).start())
    for j in range(J):
        exchange(1, j).start()
        exchange(2, j).start()
    for j in range(J):
        exchange(0, j).start()

    def conv(a, h):
        cols = pl.ds(pl.multiple_of(h * DH, DH), DH)
        taps = taps_all[a, :, cols]
        data = x_all[a, :, cols].astype(jnp.float32)
        total = taps[0:1] * data[RIM:]
        for j in range(1, KC):
            total = total + taps[j : j + 1] * pltpu.roll(data, j, 0)[RIM:]
        return total.astype(jnp.bfloat16)

    def s_copy(j, o):
        return pltpu.make_async_remote_copy(
            s_send.at[j, o], s_recv.at[j, me], ss_sem.at[j, o], sr_sem.at[j, me],
            device_id=member(o), device_id_type=MESH,
        )

    def s_arrival(j, g):
        return pltpu.make_async_remote_copy(
            s_send.at[j, g], s_recv.at[j, g], ss_sem.at[j, g], sr_sem.at[j, g],
            device_id=member(g), device_id_type=MESH,
        )

    def r_copy(j, g):
        return pltpu.make_async_remote_copy(
            r_send.at[j, g], r_recv.at[j, me], rs_sem.at[j, g], rr_sem.at[j, me],
            device_id=member(g), device_id_type=MESH,
        )

    def r_arrival(j, o):
        return pltpu.make_async_remote_copy(
            r_send.at[j, o], r_recv.at[j, o], rs_sem.at[j, o], rr_sem.at[j, o],
            device_id=member(o), device_id_type=MESH,
        )

    def chain(j):
        return pltpu.make_async_remote_copy(
            chain_out.at[j], chain_in.at[j], cs_sem.at[j], cr_sem.at[j],
            device_id=(c + X, hd), device_id_type=MESH,
        )

    def keys_and_sums(j, o):
        h = j * G + o
        k = conv(1, h)
        v = conv(2, h)
        wide_k = k.astype(jnp.float32)
        norm = jnp.sum(wide_k * wide_k, axis=1, keepdims=True) * (0.5 * scale * scale)
        part = jnp.dot(k, omega[h], preferred_element_type=jnp.float32)
        feats = jnp.exp(part * scale - norm).astype(jnp.bfloat16)
        kf[h] = feats
        vals[h] = v
        joined = jnp.concatenate([v, jnp.ones_like(v)], axis=1)
        sums = lax.dot_general(
            joined, feats, (((0,), (0,)), ((), ())), preferred_element_type=jnp.float32
        )
        sums = jnp.concatenate(
            [sums[:DH, :DH], sums[:DH, DH:], sums[DH : DH + 8, :DH], sums[DH : DH + 8, DH:]], axis=0
        ).astype(jnp.bfloat16)

        @pl.when(o == me)
        def _():
            s_recv[j, o] = sums

        @pl.when(o != me)
        def _():
            s_send[j, o] = sums
            s_copy(j, o).start()

    def own(j):
        def await_sums(g, _):
            pl.when(g != me)(lambda: s_arrival(j, g).wait_recv())
            return 0

        lax.fori_loop(0, G, await_sums, 0)
        total = s_recv[j, 0].astype(jnp.float32)
        for g in range(1, G):
            total = total + s_recv[j, g].astype(jnp.float32)

        @pl.when(z == 0)
        def _():
            chain_in[j] = jnp.zeros((SROWS, DH), jnp.bfloat16)

        @pl.when(z > 0)
        def _():
            chain(j).wait_recv()

        before = chain_in[j].astype(jnp.float32)

        @pl.when(z < Z - 1)
        def _():
            chain_out[j] = (before + total).astype(jnp.bfloat16)
            chain(j).start()

        running = before
        for g in range(G):
            piece = running.astype(jnp.bfloat16)

            @pl.when(g == me)
            def _():
                r_recv[j, g] = piece

            @pl.when(g != me)
            def _():
                r_send[j, g] = piece
                r_copy(j, g).start()

            if g < G - 1:
                running = running + s_recv[j, g].astype(jnp.float32)

    def within(j, o):
        h = j * G + o
        q = conv(0, h)
        part = jnp.dot(q, omega[h], preferred_element_type=jnp.float32)
        feats = jnp.exp(part * scale).astype(jnp.bfloat16)
        qf[h] = feats
        scores = lax.dot_general(
            feats, kf[h], (((1,), (1,)), ((), ())), preferred_element_type=jnp.float32
        )
        at = lax.broadcasted_iota(jnp.int32, (T, T), 0)
        of = lax.broadcasted_iota(jnp.int32, (T, T), 1)
        scores = jnp.where(at >= of, scores, 0.0).astype(jnp.bfloat16)
        v = vals[h]
        joined = jnp.concatenate([v, jnp.ones_like(v)], axis=1)
        intra[h] = jnp.dot(scores, joined, preferred_element_type=jnp.float32)

    def finish(j, o):
        h = j * G + o
        pl.when(o != me)(lambda: r_arrival(j, o).wait_recv())
        state = r_recv[j, o]
        weights = state[2 * DH :].astype(jnp.float32)
        weights = jnp.concatenate([weights[:8], weights[8:]], axis=1)
        weights = jnp.concatenate([weights, weights], axis=0).astype(jnp.bfloat16)
        sums = jnp.concatenate([state[:DH], state[DH : 2 * DH]], axis=1)
        joined = jnp.concatenate([sums] + [weights] * (DH // 16), axis=0)
        both = intra[h] + lax.dot_general(
            qf[h], joined, (((1,), (1,)), ((), ())), preferred_element_type=jnp.float32
        )
        result = (both[:, :DH] / both[:, DH:]).astype(jnp.bfloat16)
        outb[:, pl.ds(pl.multiple_of(h * DH, DH), DH)] = result

    def out_cols(j):
        return pl.ds(pl.multiple_of(j * wide, wide), wide)

    def out_remote(j):
        return pltpu.make_async_remote_copy(
            outb.at[pl.ds(pl.multiple_of(other * rows, rows), rows), out_cols(j)],
            out.at[:, pl.ds(pl.multiple_of(core * half + j * wide, wide), wide)],
            os_sem.at[j], or_sem.at[j], device_id=mate, device_id_type=MESH,
        )

    def out_local(j):
        return pltpu.make_async_copy(
            outb.at[pl.ds(pl.multiple_of(core * rows, rows), rows), out_cols(j)],
            out.at[:, pl.ds(pl.multiple_of(core * half + j * wide, wide), wide)],
            ol_sem.at[j],
        )

    def over(count, body):
        def step(i, _):
            body(i)
            return 0

        lax.fori_loop(0, count, step, 0)

    def ordered(i):
        return lax.rem(x + 1 + i, X) * Y + lax.rem(y + 1 + i // X, Y)

    taps_copy.wait()
    omega_copy.wait()
    load(1).wait()
    load(2).wait()
    load(0).wait()
    pl.when(has_prev)(lambda: rim(0).wait_recv())
    edge = rim_in[...].astype(jnp.float32)
    for a in range(3):
        moved = pltpu.roll(edge, 3 * a, 0) if a else edge
        x_all[a, pl.ds(0, RIM), :] = moved.astype(x_all.dtype)

    def first(j):
        exchange(1, j).wait_recv()
        exchange(2, j).wait_recv()
        over(G, lambda i: keys_and_sums(j, ordered(i)))

    over(J, first)

    def middle(j):
        own(j)
        exchange(0, j).wait_recv()
        over(G, lambda o: within(j, o))

    over(J, middle)

    def last(j):
        over(G, lambda o: finish(j, o))
        out_remote(j).start()
        out_local(j).start()

    over(J, last)

    for k in range(CORES):
        pl.when(has_next)(lambda k=k: rim(k).wait_send())

    def drain(j):
        for a in range(3):
            exchange(a, j).wait_send()

        def one(g):
            @pl.when(g != me)
            def _():
                s_copy(j, g).wait_send()
                r_copy(j, g).wait_send()

        over(G, one)
        pl.when(z < Z - 1)(lambda: chain(j).wait_send())
        out_remote(j).wait()
        out_local(j).wait()

    over(J, drain)


def plan_of(ctx_size, head_size):
    along_x = 1
    while along_x * along_x * 4 <= ctx_size:
        along_x *= 2
    return along_x, head_size // CORES, ctx_size // along_x


def per_device(projected, conv_filter, frequencies):
    plan = plan_of(lax.axis_size("ctx"), lax.axis_size("head"))
    rows, width = projected.shape[1], projected.shape[2]
    half = width // CORES
    heads = half // DH
    group = plan[0] * plan[1]
    slots = heads // group
    T = CORES * rows
    bf16 = jnp.bfloat16
    dma = pltpu.SemaphoreType.DMA
    return pl.pallas_call(
        functools.partial(kernel, plan),
        out_shape=jax.ShapeDtypeStruct((rows, width), bf16),
        in_specs=[
            pl.BlockSpec(memory_space=pl.ANY),
            pl.BlockSpec(memory_space=pl.ANY),
            pl.BlockSpec(memory_space=pl.ANY),
        ],
        out_specs=pl.BlockSpec(memory_space=pl.ANY),
        scratch_shapes=[
            pltpu.VMEM((3, RIM + T, half), bf16),
            pltpu.VMEM((3, RIM, width), bf16),
            pltpu.VMEM((RIM, width), bf16),
            pltpu.VMEM((RIM, half), bf16),
            pltpu.VMEM((3, KC, half), jnp.float32),
            pltpu.VMEM((heads, DH, M), bf16),
            pltpu.VMEM((heads, T, M), bf16),
            pltpu.VMEM((heads, T, DH), bf16),
            pltpu.VMEM((heads, T, M), bf16),
            pltpu.VMEM((heads, T, 2 * DH), jnp.float32),
            pltpu.VMEM((slots, group, SROWS, DH), bf16),
            pltpu.VMEM((slots, group, SROWS, DH), bf16),
            pltpu.VMEM((slots, SROWS, DH), bf16),
            pltpu.VMEM((slots, SROWS, DH), bf16),
            pltpu.VMEM((slots, group, SROWS, DH), bf16),
            pltpu.VMEM((slots, group, SROWS, DH), bf16),
            pltpu.VMEM((T, half), bf16),
            dma((3,)), dma, dma, dma, dma((3, slots)), dma((3, slots)), dma((CORES,)), dma,
            dma((slots, group)), dma((slots, group)),
            dma((slots,)), dma((slots,)),
            dma((slots, group)), dma((slots, group)),
            dma((slots,)), dma((slots,)), dma((slots,)),
        ],
        compiler_params=pltpu.CompilerParams(
            collective_id=0, has_side_effects=True, vmem_limit_bytes=60 * 1024 * 1024
        ),
        cost_estimate=pl.CostEstimate(
            flops=2_000_000_000, bytes_accessed=8_000_000, transcendentals=2_000_000
        ),
    )(projected, conv_filter, frequencies)


def solution(mesh):
    placed = (P(None, ("ctx", "head"), None), P(), P())
    return jax.shard_map(
        per_device, mesh=mesh, in_specs=placed, out_specs=P(("ctx", "head"), None), check_vma=False
    )
```

```python
import functools

import jax
import jax.numpy as jnp
from jax import lax
from jax.experimental import pallas as pl
from jax.experimental.pallas import tpu as pltpu
from jax.sharding import PartitionSpec as P

DH = 128
M = 256
KC = 4
CORES = 2
RIM = 16
SROWS = 2 * DH + 16
MESH = pl.DeviceIdType.MESH


def kernel(
    plan,
    proj, filt, freq, out,
    x_all, tail, packed, rim_in, taps_all, omega, kf, vals, qf, intra, s_send, s_recv, chain_in, chain_out, r_send, r_recv, outb,
    load_sem, freq_sem, filt_sem, tail_sem, ex_send, ex_recv, rim_send, rim_recv,
    ss_sem, sr_sem, cs_sem, cr_sem, rs_sem, rr_sem, os_sem, or_sem, ol_sem,
):
    X, Y, Z = plan
    G = X * Y
    rows = proj.shape[1]
    half = proj.shape[2] // CORES
    J = half // DH // G
    T = CORES * rows
    wide = G * DH
    scale = DH ** (-0.25)

    c = lax.axis_index("ctx")
    hd = lax.axis_index("head")
    y, core = hd // CORES, hd % CORES
    z, x = c // X, c % X
    me = x * Y + y
    other = 1 - core
    chip = c * Y + y
    chips = X * Y * Z

    def member(g):
        return (z * X + g // Y, (g % Y) * CORES + core)

    def at_chip(n, k):
        return (n // Y, (n % Y) * CORES + k)

    mate = (c, y * CORES + other)
    has_next = (core == 1) & (chip < chips - 1)
    has_prev = chip > 0

    barrier = pltpu.get_barrier_semaphore()

    def greet(dev):
        pl.semaphore_signal(barrier, inc=1, device_id=dev, device_id_type=MESH)

    greet(mate)
    for g in range(G):
        pl.when(g != me)(lambda g=g: greet(member(g)))
    pl.when(z > 0)(lambda: greet((c - X, hd)))
    pl.when(z < Z - 1)(lambda: greet((c + X, hd)))
    for k in range(CORES):
        pl.when(has_next)(lambda k=k: greet(at_chip(chip + 1, k)))
    pl.when(has_prev)(lambda: greet(at_chip(chip - 1, 1)))

    my_cols = pl.ds(pl.multiple_of(core * half, half), half)
    my_rows = pl.ds(pl.multiple_of(RIM + core * rows, 16), rows)

    def load(a):
        return pltpu.make_async_copy(
            proj.at[a, :, my_cols], x_all.at[a, my_rows, :], load_sem.at[a]
        )

    def exchange(a, j):
        far = pl.ds(pl.multiple_of(other * half + j * wide, wide), wide)
        near = pl.ds(pl.multiple_of(j * wide, wide), wide)
        return pltpu.make_async_remote_copy(
            proj.at[a, :, far], x_all.at[a, my_rows, near],
            ex_send.at[a, j], ex_recv.at[a, j], device_id=mate, device_id_type=MESH,
        )

    def rim(k):
        return pltpu.make_async_remote_copy(
            packed.at[:, pl.ds(k * half, half)], rim_in,
            rim_send.at[k], rim_recv,
            device_id=at_chip(chip + 1, k), device_id_type=MESH,
        )

    tail_copy = pltpu.make_async_copy(proj.at[:, pl.ds(rows - RIM, RIM), :], tail, tail_sem)
    taps_copy = pltpu.make_async_copy(filt.at[:, :, my_cols], taps_all, filt_sem)

    omega_copy = pltpu.make_async_copy(
        freq.at[pl.ds(core * (half // DH), half // DH)], omega, freq_sem
    )
    pl.when(has_next)(tail_copy.start)
    load(1).start()
    load(2).start()
    taps_copy.start()
    omega_copy.start()
    load(0).start()

    @pl.when(has_next)
    def _():
        tail_copy.wait()
        row = lax.broadcasted_iota(jnp.int32, (RIM, half), 0)
        for k in range(CORES):
            parts = [tail[a, :, pl.ds(k * half, half)].astype(jnp.float32) for a in range(3)]
            both = jnp.where(row >= RIM - 6, pltpu.roll(parts[1], RIM - 3, 0), pltpu.roll(parts[2], RIM - 6, 0))
            joined = jnp.where(row >= RIM - 3, parts[0], both)
            packed[:, pl.ds(k * half, half)] = joined.astype(packed.dtype)

    @pl.when(jnp.logical_not(has_prev))
    def _():
        rim_in[...] = jnp.zeros((RIM, half), rim_in.dtype)

    greeted = (
        G + (z > 0).astype(jnp.int32) + (z < Z - 1).astype(jnp.int32)
        + CORES * has_next.astype(jnp.int32) + has_prev.astype(jnp.int32)
    )
    pl.semaphore_wait(barrier, greeted)

    for k in range(CORES):
        pl.when(has_next)(lambda k=k: rim(k).start())
    for j in range(J):
        exchange(1, j).start()
        exchange(2, j).start()
    for j in range(J):
        exchange(0, j).start()

    def conv(a, h):
        cols = pl.ds(pl.multiple_of(h * DH, DH), DH)
        taps = taps_all[a, :, cols]
        data = x_all[a, :, cols].astype(jnp.float32)
        total = taps[0:1] * data[RIM:]
        for j in range(1, KC):
            total = total + taps[j : j + 1] * pltpu.roll(data, j, 0)[RIM:]
        return total.astype(jnp.bfloat16)

    def s_copy(j, o):
        return pltpu.make_async_remote_copy(
            s_send.at[j, o], s_recv.at[j, me], ss_sem.at[j, o], sr_sem.at[j, me],
            device_id=member(o), device_id_type=MESH,
        )

    def s_arrival(j, g):
        return pltpu.make_async_remote_copy(
            s_send.at[j, g], s_recv.at[j, g], ss_sem.at[j, g], sr_sem.at[j, g],
            device_id=member(g), device_id_type=MESH,
        )

    def r_copy(j, g):
        return pltpu.make_async_remote_copy(
            r_send.at[j, g], r_recv.at[j, me], rs_sem.at[j, g], rr_sem.at[j, me],
            device_id=member(g), device_id_type=MESH,
        )

    def r_arrival(j, o):
        return pltpu.make_async_remote_copy(
            r_send.at[j, o], r_recv.at[j, o], rs_sem.at[j, o], rr_sem.at[j, o],
            device_id=member(o), device_id_type=MESH,
        )

    def chain(j):
        return pltpu.make_async_remote_copy(
            chain_out.at[j], chain_in.at[j], cs_sem.at[j], cr_sem.at[j],
            device_id=(c + X, hd), device_id_type=MESH,
        )

    def keys_and_sums(j, places):
        heads = [j * G + o for o in places]
        ks = [conv(1, h) for h in heads]
        vs = [conv(2, h) for h in heads]
        parts = [
            jnp.dot(k, omega[h], preferred_element_type=jnp.float32) for k, h in zip(ks, heads)
        ]
        wides = [k.astype(jnp.float32) for k in ks]
        norms = [
            jnp.sum(w * w, axis=1, keepdims=True) * (0.5 * scale * scale) for w in wides
        ]
        feats = [
            jnp.exp(part * scale - norm).astype(jnp.bfloat16) for part, norm in zip(parts, norms)
        ]
        sums = [
            lax.dot_general(
                jnp.concatenate([v, jnp.ones_like(v)], axis=1), f,
                (((0,), (0,)), ((), ())), preferred_element_type=jnp.float32,
            )
            for v, f in zip(vs, feats)
        ]
        for h, o, v, f, w in zip(heads, places, vs, feats, sums):
            kf[h] = f
            vals[h] = v
            s_send[j, o] = jnp.concatenate(
                [w[:DH, :DH], w[:DH, DH:], w[DH : DH + 8, :DH], w[DH : DH + 8, DH:]], axis=0
            ).astype(jnp.bfloat16)

    def own(j):
        def await_sums(g, _):
            pl.when(g != me)(lambda: s_arrival(j, g).wait_recv())
            return 0

        lax.fori_loop(0, G, await_sums, 0)
        total = s_recv[j, 0].astype(jnp.float32)
        for g in range(1, G):
            total = total + s_recv[j, g].astype(jnp.float32)

        @pl.when(z == 0)
        def _():
            chain_in[j] = jnp.zeros((SROWS, DH), jnp.bfloat16)

        @pl.when(z > 0)
        def _():
            chain(j).wait_recv()

        before = chain_in[j].astype(jnp.float32)

        @pl.when(z < Z - 1)
        def _():
            chain_out[j] = (before + total).astype(jnp.bfloat16)
            chain(j).start()

        running = before
        for g in range(G):
            piece = running.astype(jnp.bfloat16)

            @pl.when(g == me)
            def _():
                r_recv[j, g] = piece

            @pl.when(g != me)
            def _():
                r_send[j, g] = piece
                r_copy(j, g).start()

            if g < G - 1:
                running = running + s_recv[j, g].astype(jnp.float32)

    def within(heads):
        qs = [conv(0, h) for h in heads]
        keys = [kf[h] for h in heads]
        vs = [vals[h] for h in heads]
        parts = [
            jnp.dot(q, omega[h], preferred_element_type=jnp.float32) for q, h in zip(qs, heads)
        ]
        feats = [jnp.exp(part * scale).astype(jnp.bfloat16) for part in parts]
        scores = [
            lax.dot_general(f, k, (((1,), (1,)), ((), ())), preferred_element_type=jnp.float32)
            for f, k in zip(feats, keys)
        ]
        at = lax.broadcasted_iota(jnp.int32, (T, T), 0)
        of = lax.broadcasted_iota(jnp.int32, (T, T), 1)
        scores = [jnp.where(at >= of, w, 0.0).astype(jnp.bfloat16) for w in scores]
        sums = [
            jnp.dot(
                w, jnp.concatenate([v, jnp.ones_like(v)], axis=1),
                preferred_element_type=jnp.float32,
            )
            for w, v in zip(scores, vs)
        ]
        for h, f, w in zip(heads, feats, sums):
            qf[h] = f
            intra[h] = w

    def finish(j, places):
        for o in places:
            pl.when(o != me)(lambda o=o: r_arrival(j, o).wait_recv())
        heads = [j * G + o for o in places]
        joins = []
        for o in places:
            state = r_recv[j, o]
            weights = state[2 * DH :].astype(jnp.float32)
            weights = jnp.concatenate([weights[:8], weights[8:]], axis=1)
            weights = jnp.concatenate([weights, weights], axis=0).astype(jnp.bfloat16)
            sums = jnp.concatenate([state[:DH], state[DH : 2 * DH]], axis=1)
            joins.append(jnp.concatenate([sums] + [weights] * (DH // 16), axis=0))
        both = [
            intra[h] + lax.dot_general(
                qf[h], joined, (((1,), (1,)), ((), ())), preferred_element_type=jnp.float32
            )
            for h, joined in zip(heads, joins)
        ]
        results = [(b[:, :DH] / b[:, DH:]).astype(jnp.bfloat16) for b in both]
        for h, result in zip(heads, results):
            outb[:, pl.ds(pl.multiple_of(h * DH, DH), DH)] = result

    piece = wide // 2

    def out_remote(i):
        return pltpu.make_async_remote_copy(
            outb.at[
                pl.ds(pl.multiple_of(other * rows, rows), rows),
                pl.ds(pl.multiple_of(i * piece, piece), piece),
            ],
            out.at[:, pl.ds(pl.multiple_of(core * half + i * piece, piece), piece)],
            os_sem.at[i], or_sem.at[i], device_id=mate, device_id_type=MESH,
        )

    def out_local(i):
        return pltpu.make_async_copy(
            outb.at[
                pl.ds(pl.multiple_of(core * rows, rows), rows),
                pl.ds(pl.multiple_of(i * piece, piece), piece),
            ],
            out.at[:, pl.ds(pl.multiple_of(core * half + i * piece, piece), piece)],
            ol_sem.at[i],
        )

    def over(count, body):
        def step(i, _):
            body(i)
            return 0

        lax.fori_loop(0, count, step, 0)

    def ordered(i):
        return lax.rem(x + 1 + i, X) * Y + lax.rem(y + 1 + i // X, Y)

    taps_copy.wait()
    omega_copy.wait()
    load(1).wait()
    load(2).wait()
    load(0).wait()
    pl.when(has_prev)(lambda: rim(0).wait_recv())
    edge = rim_in[...].astype(jnp.float32)
    for a in range(3):
        moved = pltpu.roll(edge, 3 * a, 0) if a else edge
        x_all[a, pl.ds(0, RIM), :] = moved.astype(x_all.dtype)

    pairs = G // 4
    steps = 4 * J
    lag = jnp.minimum(z, steps - 2 * J - 2)

    def step(t):
        j = lax.rem(t // 2, J)
        low = lax.rem(t, 2) * (G // 2)

        @pl.when(t < 2 * J)
        def _():
            @pl.when(lax.rem(t, 2) == 0)
            def _():
                exchange(1, j).wait_recv()
                exchange(2, j).wait_recv()

            def one(p):
                i = low + 2 * p
                places = [ordered(i), ordered(i + 1)]
                keys_and_sums(j, places)
                s_copy(j, places[0]).start()
                pl.when(i + 1 < G - 1)(lambda: s_copy(j, places[1]).start())

            over(pairs, one)

            @pl.when(lax.rem(t, 2) == 1)
            def _():
                s_recv[j, me] = s_send[j, me]

        @pl.when(t >= 2 * J)
        def _():
            pl.when(lax.rem(t, 2) == 0)(lambda: exchange(0, j).wait_recv())

            def one(p):
                h = j * G + low + 2 * p
                within([h, h + 1])

            over(pairs, one)

        due = t - 3 - lag

        @pl.when((due >= 0) & (lax.rem(due, 2) == 0) & (due < 2 * J))
        def _():
            own(due // 2)

    over(steps, step)

    def last(i):
        j = i // 2
        low = lax.rem(i, 2) * (G // 2)

        def one(p):
            o = low + 2 * p
            finish(j, [o, o + 1])

        over(pairs, one)
        out_remote(i).start()
        out_local(i).start()

    over(2 * J, last)

    for k in range(CORES):
        pl.when(has_next)(lambda k=k: rim(k).wait_send())

    def drain(j):
        for a in range(3):
            exchange(a, j).wait_send()

        def one(g):
            @pl.when(g != me)
            def _():
                s_copy(j, g).wait_send()
                r_copy(j, g).wait_send()

        over(G, one)
        pl.when(z < Z - 1)(lambda: chain(j).wait_send())
        for i in range(2):
            out_remote(2 * j + i).wait()
            out_local(2 * j + i).wait()

    over(J, drain)


def plan_of(ctx_size, head_size):
    along_x = 1
    while along_x * along_x * 4 <= ctx_size:
        along_x *= 2
    return along_x, head_size // CORES, ctx_size // along_x


def per_device(projected, conv_filter, frequencies):
    plan = plan_of(lax.axis_size("ctx"), lax.axis_size("head"))
    rows, width = projected.shape[1], projected.shape[2]
    half = width // CORES
    heads = half // DH
    group = plan[0] * plan[1]
    slots = heads // group
    T = CORES * rows
    bf16 = jnp.bfloat16
    dma = pltpu.SemaphoreType.DMA
    return pl.pallas_call(
        functools.partial(kernel, plan),
        out_shape=jax.ShapeDtypeStruct((rows, width), bf16),
        in_specs=[pl.BlockSpec(memory_space=pltpu.HBM)] * 3,
        out_specs=pl.BlockSpec(memory_space=pl.ANY),
        scratch_shapes=[
            pltpu.VMEM((3, RIM + T, half), bf16),
            pltpu.VMEM((3, RIM, width), bf16),
            pltpu.VMEM((RIM, width), bf16),
            pltpu.VMEM((RIM, half), bf16),
            pltpu.VMEM((3, KC, half), jnp.float32),
            pltpu.VMEM((heads, DH, M), bf16),
            pltpu.VMEM((heads, T, M), bf16),
            pltpu.VMEM((heads, T, DH), bf16),
            pltpu.VMEM((heads, T, M), bf16),
            pltpu.VMEM((heads, T, 2 * DH), jnp.float32),
            pltpu.VMEM((slots, group, SROWS, DH), bf16),
            pltpu.VMEM((slots, group, SROWS, DH), bf16),
            pltpu.VMEM((slots, SROWS, DH), bf16),
            pltpu.VMEM((slots, SROWS, DH), bf16),
            pltpu.VMEM((slots, group, SROWS, DH), bf16),
            pltpu.VMEM((slots, group, SROWS, DH), bf16),
            pltpu.VMEM((T, half), bf16),
            dma((3,)), dma, dma, dma, dma((3, slots)), dma((3, slots)), dma((CORES,)), dma,
            dma((slots, group)), dma((slots, group)),
            dma((slots,)), dma((slots,)),
            dma((slots, group)), dma((slots, group)),
            dma((2 * slots,)), dma((2 * slots,)), dma((2 * slots,)),
        ],
        compiler_params=pltpu.CompilerParams(
            collective_id=0, has_side_effects=True, vmem_limit_bytes=40 * 1024 * 1024
        ),
        cost_estimate=pl.CostEstimate(
            flops=2_000_000_000, bytes_accessed=8_000_000, transcendentals=2_000_000
        ),
    )(*[pltpu.with_memory_space_constraint(a, pltpu.HBM) for a in (projected, conv_filter, frequencies)])


def solution(mesh):
    placed = (P(None, ("ctx", "head"), None), P(), P())
    return jax.shard_map(
        per_device, mesh=mesh, in_specs=placed, out_specs=P(("ctx", "head"), None), check_vma=False
    )
```

```python
import functools

import jax
import jax.numpy as jnp
from jax import lax
from jax.experimental import pallas as pl
from jax.experimental.pallas import tpu as pltpu
from jax.sharding import PartitionSpec as P

DH = 128
M = 256
KC = 4
LOG2E = 1.4426950408889634
CORES = 2
RIM = 16
SROWS = 2 * DH + 16
MESH = pl.DeviceIdType.MESH


def kernel(
    plan,
    proj, filt, freq, out,
    x_all, tail, packed, rim_in, taps_all, omega, kf, vals, qf, intra, s_send, s_recv, chain_in, chain_out, r_send, r_recv, outb,
    load_sem, freq_sem, filt_sem, tail_sem, ex_send, ex_recv, rim_send, rim_recv,
    ss_sem, sr_sem, cs_sem, cr_sem, rs_sem, rr_sem, os_sem, or_sem, ol_sem,
):
    X, Y, Z = plan
    G = X * Y
    rows = proj.shape[1]
    half = proj.shape[2] // CORES
    J = half // DH // G
    T = CORES * rows
    wide = G * DH
    scale = DH ** (-0.25)

    c = lax.axis_index("ctx")
    hd = lax.axis_index("head")
    y, core = hd // CORES, hd % CORES
    z, x = c // X, c % X
    me = x * Y + y
    other = 1 - core
    chip = c * Y + y
    chips = X * Y * Z

    def member(g):
        return (z * X + g // Y, (g % Y) * CORES + core)

    def at_chip(n, k):
        return (n // Y, (n % Y) * CORES + k)

    mate = (c, y * CORES + other)
    has_next = (core == 1) & (chip < chips - 1)
    has_prev = chip > 0

    barrier = pltpu.get_barrier_semaphore()

    def greet(dev):
        pl.semaphore_signal(barrier, inc=1, device_id=dev, device_id_type=MESH)

    greet(mate)
    for g in range(G):
        pl.when(g != me)(lambda g=g: greet(member(g)))
    pl.when(z > 0)(lambda: greet((c - X, hd)))
    pl.when(z < Z - 1)(lambda: greet((c + X, hd)))
    for k in range(CORES):
        pl.when(has_next)(lambda k=k: greet(at_chip(chip + 1, k)))
    pl.when(has_prev)(lambda: greet(at_chip(chip - 1, 1)))

    my_cols = pl.ds(pl.multiple_of(core * half, half), half)
    my_rows = pl.ds(pl.multiple_of(RIM + core * rows, 16), rows)

    def load(a):
        return pltpu.make_async_copy(
            proj.at[a, :, my_cols], x_all.at[a, my_rows, :], load_sem.at[a]
        )

    def exchange(a, j):
        far = pl.ds(pl.multiple_of(other * half + j * wide, wide), wide)
        near = pl.ds(pl.multiple_of(j * wide, wide), wide)
        return pltpu.make_async_remote_copy(
            proj.at[a, :, far], x_all.at[a, my_rows, near],
            ex_send.at[a, j], ex_recv.at[a, j], device_id=mate, device_id_type=MESH,
        )

    def rim(k):
        return pltpu.make_async_remote_copy(
            packed.at[:, pl.ds(k * half, half)], rim_in,
            rim_send.at[k], rim_recv,
            device_id=at_chip(chip + 1, k), device_id_type=MESH,
        )

    tail_copy = pltpu.make_async_copy(proj.at[:, pl.ds(rows - RIM, RIM), :], tail, tail_sem)
    taps_copy = pltpu.make_async_copy(filt.at[:, :, my_cols], taps_all, filt_sem)

    omega_copy = pltpu.make_async_copy(
        freq.at[pl.ds(core * (half // DH), half // DH)], omega, freq_sem
    )
    pl.when(has_next)(tail_copy.start)
    load(1).start()
    load(2).start()
    taps_copy.start()
    omega_copy.start()
    load(0).start()

    @pl.when(has_next)
    def _():
        tail_copy.wait()
        row = lax.broadcasted_iota(jnp.int32, (RIM, half), 0)
        for k in range(CORES):
            parts = [tail[a, :, pl.ds(k * half, half)].astype(jnp.float32) for a in range(3)]
            both = jnp.where(row >= RIM - 6, pltpu.roll(parts[1], RIM - 3, 0), pltpu.roll(parts[2], RIM - 6, 0))
            joined = jnp.where(row >= RIM - 3, parts[0], both)
            packed[:, pl.ds(k * half, half)] = joined.astype(packed.dtype)

    @pl.when(jnp.logical_not(has_prev))
    def _():
        rim_in[...] = jnp.zeros((RIM, half), rim_in.dtype)

    greeted = (
        G + (z > 0).astype(jnp.int32) + (z < Z - 1).astype(jnp.int32)
        + CORES * has_next.astype(jnp.int32) + has_prev.astype(jnp.int32)
    )
    pl.semaphore_wait(barrier, greeted)

    for k in range(CORES):
        pl.when(has_next)(lambda k=k: rim(k).start())
    for j in range(J):
        exchange(1, j).start()
        exchange(2, j).start()
    for j in range(J):
        exchange(0, j).start()

    def conv(a, h):
        cols = pl.ds(pl.multiple_of(h * DH, DH), DH)
        taps = taps_all[a, :, cols]
        data = x_all[a, :, cols].astype(jnp.float32)
        total = taps[0:1] * data[RIM:]
        for j in range(1, KC):
            total = total + taps[j : j + 1] * pltpu.roll(data, j, 0)[RIM:]
        return total.astype(jnp.bfloat16)

    def s_copy(j, o):
        return pltpu.make_async_remote_copy(
            s_send.at[j, o], s_recv.at[j, me], ss_sem.at[j, o], sr_sem.at[j, me],
            device_id=member(o), device_id_type=MESH,
        )

    def s_arrival(j, g):
        return pltpu.make_async_remote_copy(
            s_send.at[j, g], s_recv.at[j, g], ss_sem.at[j, g], sr_sem.at[j, g],
            device_id=member(g), device_id_type=MESH,
        )

    def r_copy(j, g):
        return pltpu.make_async_remote_copy(
            r_send.at[j, g], r_recv.at[j, me], rs_sem.at[j, g], rr_sem.at[j, me],
            device_id=member(g), device_id_type=MESH,
        )

    def r_arrival(j, o):
        return pltpu.make_async_remote_copy(
            r_send.at[j, o], r_recv.at[j, o], rs_sem.at[j, o], rr_sem.at[j, o],
            device_id=member(o), device_id_type=MESH,
        )

    def chain(j):
        return pltpu.make_async_remote_copy(
            chain_out.at[j], chain_in.at[j], cs_sem.at[j], cr_sem.at[j],
            device_id=(c + X, hd), device_id_type=MESH,
        )

    def keys_and_sums(j, places):
        heads = [j * G + o for o in places]
        ks = [conv(1, h) for h in heads]
        vs = [conv(2, h) for h in heads]
        parts = [
            jnp.dot(k, omega[h], preferred_element_type=jnp.float32) for k, h in zip(ks, heads)
        ]
        wides = [k.astype(jnp.float32) for k in ks]
        norms = [
            jnp.sum(w * w, axis=1, keepdims=True) * (0.5 * scale * scale * LOG2E) for w in wides
        ]
        feats = [
            jnp.exp2(part * (scale * LOG2E) - norm).astype(jnp.bfloat16)
            for part, norm in zip(parts, norms)
        ]
        sums = [
            jnp.dot(
                jnp.concatenate([v.T, jnp.ones((16, T), v.dtype)], axis=0), f,
                preferred_element_type=jnp.float32,
            )
            for v, f in zip(vs, feats)
        ]
        for h, o, v, f, w in zip(heads, places, vs, feats, sums):
            kf[h] = f
            vals[h] = v
            s_send[j, o] = jnp.concatenate(
                [w[:DH, :DH], w[:DH, DH:], w[DH : DH + 8, :DH], w[DH : DH + 8, DH:]], axis=0
            ).astype(jnp.bfloat16)

    def own(j):
        def await_sums(g, _):
            pl.when(g != me)(lambda: s_arrival(j, g).wait_recv())
            return 0

        lax.fori_loop(0, G, await_sums, 0)
        total = s_recv[j, 0].astype(jnp.float32)
        for g in range(1, G):
            total = total + s_recv[j, g].astype(jnp.float32)

        @pl.when(z == 0)
        def _():
            chain_in[j] = jnp.zeros((SROWS, DH), jnp.bfloat16)

        @pl.when(z > 0)
        def _():
            chain(j).wait_recv()

        before = chain_in[j].astype(jnp.float32)

        @pl.when(z < Z - 1)
        def _():
            chain_out[j] = (before + total).astype(jnp.bfloat16)
            chain(j).start()

        running = before
        for g in range(G):
            piece = running.astype(jnp.bfloat16)

            @pl.when(g == me)
            def _():
                r_recv[j, g] = piece

            @pl.when(g != me)
            def _():
                r_send[j, g] = piece
                r_copy(j, g).start()

            if g < G - 1:
                running = running + s_recv[j, g].astype(jnp.float32)

    def within(heads):
        qs = [conv(0, h) for h in heads]
        keys = [kf[h] for h in heads]
        vs = [vals[h] for h in heads]
        parts = [
            jnp.dot(q, omega[h], preferred_element_type=jnp.float32) for q, h in zip(qs, heads)
        ]
        feats = [jnp.exp2(part * (scale * LOG2E)).astype(jnp.bfloat16) for part in parts]
        scores = [
            lax.dot_general(f, k, (((1,), (1,)), ((), ())), preferred_element_type=jnp.float32)
            for f, k in zip(feats, keys)
        ]
        at = lax.broadcasted_iota(jnp.int32, (rows, rows), 0)
        of = lax.broadcasted_iota(jnp.int32, (rows, rows), 1)
        causal = at >= of
        never = jnp.zeros((rows, rows), jnp.bfloat16)

        def masked(w):
            first = jnp.where(causal, w[:rows, :rows], 0.0).astype(jnp.bfloat16)
            second = jnp.where(causal, w[rows:, rows:], 0.0).astype(jnp.bfloat16)
            under = w[rows:, :rows].astype(jnp.bfloat16)
            return jnp.concatenate(
                [jnp.concatenate([first, never], axis=1), jnp.concatenate([under, second], axis=1)],
                axis=0,
            )

        scores = [masked(w) for w in scores]
        sums = [
            jnp.dot(
                w, jnp.concatenate([v, jnp.ones_like(v)], axis=1),
                preferred_element_type=jnp.float32,
            )
            for w, v in zip(scores, vs)
        ]
        for h, f, w in zip(heads, feats, sums):
            qf[h] = f
            intra[h] = w

    def finish(j, places):
        for o in places:
            pl.when(o != me)(lambda o=o: r_arrival(j, o).wait_recv())
        heads = [j * G + o for o in places]
        joins = []
        for o in places:
            state = r_recv[j, o]
            weights = state[2 * DH :].astype(jnp.float32)
            weights = jnp.concatenate([weights[:8], weights[8:]], axis=1)
            weights = jnp.concatenate([weights, weights], axis=0).astype(jnp.bfloat16)
            sums = jnp.concatenate([state[:DH], state[DH : 2 * DH]], axis=1)
            joins.append(jnp.concatenate([sums] + [weights] * (DH // 16), axis=0))
        both = [
            intra[h] + lax.dot_general(
                qf[h], joined, (((1,), (1,)), ((), ())), preferred_element_type=jnp.float32
            )
            for h, joined in zip(heads, joins)
        ]
        results = [(b[:, :DH] / b[:, DH:]).astype(jnp.bfloat16) for b in both]
        for h, result in zip(heads, results):
            outb[:, pl.ds(pl.multiple_of(h * DH, DH), DH)] = result

    piece = wide // 2

    def out_remote(i):
        return pltpu.make_async_remote_copy(
            outb.at[
                pl.ds(pl.multiple_of(other * rows, rows), rows),
                pl.ds(pl.multiple_of(i * piece, piece), piece),
            ],
            out.at[:, pl.ds(pl.multiple_of(core * half + i * piece, piece), piece)],
            os_sem.at[i], or_sem.at[i], device_id=mate, device_id_type=MESH,
        )

    def out_local(i):
        return pltpu.make_async_copy(
            outb.at[
                pl.ds(pl.multiple_of(core * rows, rows), rows),
                pl.ds(pl.multiple_of(i * piece, piece), piece),
            ],
            out.at[:, pl.ds(pl.multiple_of(core * half + i * piece, piece), piece)],
            ol_sem.at[i],
        )

    def over(count, body):
        def step(i, _):
            body(i)
            return 0

        lax.fori_loop(0, count, step, 0)

    def ordered(i):
        return lax.rem(x + 1 + i, X) * Y + lax.rem(y + 1 + i // X, Y)

    taps_copy.wait()
    omega_copy.wait()
    load(1).wait()
    load(2).wait()
    load(0).wait()
    pl.when(has_prev)(lambda: rim(0).wait_recv())
    edge = rim_in[...].astype(jnp.float32)
    for a in range(3):
        moved = pltpu.roll(edge, 3 * a, 0) if a else edge
        x_all[a, pl.ds(0, RIM), :] = moved.astype(x_all.dtype)

    pairs = G // 4
    steps = 4 * J
    lag = jnp.minimum(2 * z, steps - 2 * J - 2)

    def step(t):
        j = lax.rem(t // 2, J)
        low = lax.rem(t, 2) * (G // 2)

        @pl.when(t < 2 * J)
        def _():
            @pl.when(lax.rem(t, 2) == 0)
            def _():
                exchange(1, j).wait_recv()
                exchange(2, j).wait_recv()

            def one(p):
                i = low + 2 * p
                places = [ordered(i), ordered(i + 1)]
                keys_and_sums(j, places)
                s_copy(j, places[0]).start()
                pl.when(i + 1 < G - 1)(lambda: s_copy(j, places[1]).start())

            over(pairs, one)

            @pl.when(lax.rem(t, 2) == 1)
            def _():
                s_recv[j, me] = s_send[j, me]

        @pl.when(t >= 2 * J)
        def _():
            pl.when(lax.rem(t, 2) == 0)(lambda: exchange(0, j).wait_recv())

            def one(p):
                h = j * G + low + 2 * p
                within([h, h + 1])

            over(pairs, one)

        due = t - 3 - lag

        @pl.when((due >= 0) & (lax.rem(due, 2) == 0) & (due < 2 * J))
        def _():
            own(due // 2)

    over(steps, step)

    def last(i):
        j = i // 2
        low = lax.rem(i, 2) * (G // 2)

        def one(p):
            o = low + 2 * p
            finish(j, [o, o + 1])

        over(pairs, one)
        out_remote(i).start()
        out_local(i).start()

    over(2 * J, last)

    for k in range(CORES):
        pl.when(has_next)(lambda k=k: rim(k).wait_send())

    def drain(j):
        for a in range(3):
            exchange(a, j).wait_send()

        def one(g):
            @pl.when(g != me)
            def _():
                s_copy(j, g).wait_send()
                r_copy(j, g).wait_send()

        over(G, one)
        pl.when(z < Z - 1)(lambda: chain(j).wait_send())
        for i in range(2):
            out_remote(2 * j + i).wait()
            out_local(2 * j + i).wait()

    over(J, drain)


def plan_of(ctx_size, head_size):
    along_x = 1
    while along_x * along_x * 4 <= ctx_size:
        along_x *= 2
    return along_x, head_size // CORES, ctx_size // along_x


def per_device(projected, conv_filter, frequencies):
    plan = plan_of(lax.axis_size("ctx"), lax.axis_size("head"))
    rows, width = projected.shape[1], projected.shape[2]
    half = width // CORES
    heads = half // DH
    group = plan[0] * plan[1]
    slots = heads // group
    T = CORES * rows
    bf16 = jnp.bfloat16
    dma = pltpu.SemaphoreType.DMA
    return pl.pallas_call(
        functools.partial(kernel, plan),
        out_shape=jax.ShapeDtypeStruct((rows, width), bf16),
        in_specs=[pl.BlockSpec(memory_space=pltpu.HBM)] * 3,
        out_specs=pl.BlockSpec(memory_space=pl.ANY),
        scratch_shapes=[
            pltpu.VMEM((3, RIM + T, half), bf16),
            pltpu.VMEM((3, RIM, width), bf16),
            pltpu.VMEM((RIM, width), bf16),
            pltpu.VMEM((RIM, half), bf16),
            pltpu.VMEM((3, KC, half), jnp.float32),
            pltpu.VMEM((heads, DH, M), bf16),
            pltpu.VMEM((heads, T, M), bf16),
            pltpu.VMEM((heads, T, DH), bf16),
            pltpu.VMEM((heads, T, M), bf16),
            pltpu.VMEM((heads, T, 2 * DH), jnp.float32),
            pltpu.VMEM((slots, group, SROWS, DH), bf16),
            pltpu.VMEM((slots, group, SROWS, DH), bf16),
            pltpu.VMEM((slots, SROWS, DH), bf16),
            pltpu.VMEM((slots, SROWS, DH), bf16),
            pltpu.VMEM((slots, group, SROWS, DH), bf16),
            pltpu.VMEM((slots, group, SROWS, DH), bf16),
            pltpu.VMEM((T, half), bf16),
            dma((3,)), dma, dma, dma, dma((3, slots)), dma((3, slots)), dma((CORES,)), dma,
            dma((slots, group)), dma((slots, group)),
            dma((slots,)), dma((slots,)),
            dma((slots, group)), dma((slots, group)),
            dma((2 * slots,)), dma((2 * slots,)), dma((2 * slots,)),
        ],
        compiler_params=pltpu.CompilerParams(
            collective_id=0, has_side_effects=True, vmem_limit_bytes=40 * 1024 * 1024
        ),
        cost_estimate=pl.CostEstimate(
            flops=2_000_000_000, bytes_accessed=8_000_000, transcendentals=2_000_000
        ),
    )(*[pltpu.with_memory_space_constraint(a, pltpu.HBM) for a in (projected, conv_filter, frequencies)])


def solution(mesh):
    placed = (P(None, ("ctx", "head"), None), P(), P())
    return jax.shard_map(
        per_device, mesh=mesh, in_specs=placed, out_specs=P(("ctx", "head"), None), check_vma=False
    )
```
